256 devices in a mesh: gen: 32 (over y, x, core), beam: 8 (over z).
Axes of the slice: x: 4, y: 4, z: 8, core: 2. Of those that a mesh axis runs over, the one named last changes fastest.
Arguments:
- gen_showers: bfloat16 [32768, 256], P('gen'), may hold values from -12 to 12
- beam_showers: bfloat16 [16384, 256], P('beam'), may hold values from -6 to 6
- embed_weight: bfloat16 [256, 128], replicated, may hold values from -0.375 to 0.375
- eps_roster: float32 [4], replicated, may hold values from 0.04 to 0.08
Outputs:
- gen_potential: float32 [32768], P('gen')
- beam_potential: float32 [16384], P('beam')
- weight_grad: float32 [256, 128], replicated
The draws below stay inside these ranges and needn't reach their ends.
All inputs are finite; a program needn't handle non-finite values.
Results may differ from the reference program's by a relative error of at most 0.03.
Values sent between devices are 32-bit elements; how exact they have to be, the bound alone decides.
No kernel may reach another device: no remote copies, remote signals or barrier semaphores. Data moves between devices by JAX's collectives and lax.ppermute only.
A program may use at most 64 MiB of HBM per device.

```python
import math
import jax
import jax.numpy as jnp
from jax import lax

F = 256
E = 128
SWEEPS = 4
GEN_DEV = 1024
NG = 32768
NB = 16384
N_GEN = 32


def block_scale(stream_key, dims, cuts, smallest, high):
    factor_of, own = 1.0, jax.random.fold_in(stream_key, 6)
    for position, shards_of in cuts:
        steps = jnp.exp(jax.random.uniform(jax.random.fold_in(own, position), (shards_of,), jnp.float32, smallest / len(cuts), high / len(cuts)))
        factor_of = factor_of * jnp.repeat(steps, dims[position] // shards_of).reshape([-1 if axis == position else 1 for axis in range(len(dims))])
    return factor_of


def noise(key, extent, scale, bound, cuts=(), kind=jnp.bfloat16):
    entries = scale * jax.random.normal(key, extent, jnp.float32)
    if cuts:
        entries = entries * block_scale(key, extent, cuts, -0.22, 0.18)
    return jnp.clip(entries, -bound, bound).astype(kind)


def setup_inputs(seed: int = 0) -> dict:
    key_list = jax.random.split(jax.random.key(seed), 5)
    gen_showers = noise(key_list[0], (NG, F), 2.0, 12.0, ((0, 32),))
    beam_showers = noise(key_list[1], (NB, F), 1.0, 6.0, ((0, 8),))
    embed_weight = noise(key_list[2], (F, E), F ** -0.5, 0.375)
    eps_roster = jnp.clip(jnp.exp(jax.random.uniform(key_list[3], (SWEEPS,), jnp.float32, math.log(0.04), math.log(0.08))), 0.04, 0.08)
    return dict(gen_showers=gen_showers, beam_showers=beam_showers, embed_weight=embed_weight, eps_roster=eps_roster)


def embed(showers, weight):
    act = jnp.tanh(jnp.dot(showers, weight, preferred_element_type=jnp.float32))
    return act, act.astype(jnp.bfloat16)


def cost_block(gen_emb, beam_emb, gen_sq, beam_sq):
    cross = jnp.dot(gen_emb, beam_emb.T, preferred_element_type=jnp.float32)
    return gen_sq[:, None] + beam_sq[None, :] - 2.0 * cross


def reference(gen_showers, beam_showers, embed_weight, eps_roster):
    gen_act, gen_emb = embed(gen_showers, embed_weight)
    beam_act, beam_emb = embed(beam_showers, embed_weight)
    gen_float = gen_emb.astype(jnp.float32)
    beam_float = beam_emb.astype(jnp.float32)
    gen_sq = jnp.sum(gen_float * gen_float, axis=1)
    beam_sq = jnp.sum(beam_float * beam_float, axis=1)
    emb_blocks = gen_emb.reshape(N_GEN, GEN_DEV, E)
    sq_blocks = gen_sq.reshape(N_GEN, GEN_DEV)
    act_blocks = gen_act.reshape(N_GEN, GEN_DEV, E)
    log_beam = math.log(NB)
    log_gen = math.log(NG)
    beam_pot = jnp.zeros((NB,), jnp.float32)
    gen_pot = jnp.zeros((NG,), jnp.float32)
    for sweep in range(SWEEPS):
        temper = eps_roster[sweep]

        def row_pass(pieces):
            emb_blk, sq_blk = pieces
            scores = (beam_pot[None, :] - cost_block(emb_blk, beam_emb, sq_blk, beam_sq)) / temper
            top = jnp.max(scores, axis=1)
            lse = top + jnp.log(jnp.sum(jnp.exp(scores - top[:, None]), axis=1))
            return temper * (log_beam - lse)

        gen_pot = lax.map(row_pass, (emb_blocks, sq_blocks)).reshape(NG)
        pot_blocks = gen_pot.reshape(N_GEN, GEN_DEV)

        def col_step(carry, pieces):
            top, total = carry
            emb_blk, sq_blk, pot_blk = pieces
            scores = (pot_blk[:, None] - cost_block(emb_blk, beam_emb, sq_blk, beam_sq)) / temper
            new_top = jnp.maximum(top, jnp.max(scores, axis=0))
            total = total * jnp.exp(top - new_top) + jnp.sum(jnp.exp(scores - new_top[None, :]), axis=0)
            return (new_top, total), None

        start = (jnp.full((NB,), -jnp.inf, jnp.float32), jnp.zeros((NB,), jnp.float32))
        (top, total), unused = lax.scan(col_step, start, (emb_blocks, sq_blocks, pot_blocks))
        beam_pot = temper * (log_gen - (top + jnp.log(total)))
    last = eps_roster[SWEEPS - 1]
    pot_blocks = gen_pot.reshape(N_GEN, GEN_DEV)

    def grad_step(carry, pieces):
        beam_acc, mass_acc = carry
        emb_blk, sq_blk, pot_blk, act_blk = pieces
        cost = cost_block(emb_blk, beam_emb, sq_blk, beam_sq)
        mass = jnp.exp((pot_blk[:, None] + beam_pot[None, :] - cost) / last - log_beam)
        plan = mass.astype(jnp.bfloat16)
        row_mass = jnp.sum(mass, axis=1)
        moved = jnp.dot(plan, beam_emb, preferred_element_type=jnp.float32)
        grad_rows = 2.0 * (row_mass[:, None] * emb_blk.astype(jnp.float32) - moved)
        pre_rows = grad_rows * (1.0 - act_blk * act_blk)
        beam_acc = beam_acc + jnp.dot(plan.T, emb_blk, preferred_element_type=jnp.float32)
        mass_acc = mass_acc + jnp.sum(mass, axis=0)
        return (beam_acc, mass_acc), pre_rows

    start = (jnp.zeros((NB, E), jnp.float32), jnp.zeros((NB,), jnp.float32))
    (beam_acc, col_mass), pre_blocks = lax.scan(grad_step, start, (emb_blocks, sq_blocks, pot_blocks, act_blocks))
    pre_gen = pre_blocks.reshape(NG, E)
    grad_beam = 2.0 * (col_mass[:, None] * beam_float - beam_acc)
    pre_beam = grad_beam * (1.0 - beam_act * beam_act)
    weight_grad = jnp.dot(gen_showers.astype(jnp.float32).T, pre_gen, precision=lax.Precision.HIGHEST)
    weight_grad = weight_grad + jnp.dot(beam_showers.astype(jnp.float32).T, pre_beam, precision=lax.Precision.HIGHEST)
    return gen_pot, beam_pot, weight_grad
```

```python
import functools
import math

import jax
import jax.numpy as jnp
from jax import lax
from jax.experimental import pallas as pl
from jax.experimental.pallas import tpu as pltpu
from jax.sharding import PartitionSpec as P

SWEEPS = 4
LOG2E = 1.4426950408889634
BYTES = 24 * 1024 * 1024
NT = (((1,), (1,)), ((), ()))
WIDE = 512
F32 = jnp.float32
BF16 = jnp.bfloat16


def merged(parts, scale):
    count = parts.shape[0]
    top = parts[0]
    for d in range(1, count):
        top = jnp.maximum(top, parts[d])
    total = jnp.exp2((parts[0] - top) * scale)
    for d in range(1, count):
        total = total + jnp.exp2((parts[d] - top) * scale)
    return top + jnp.log2(total) / scale


def as_column(dense):
    turned = jnp.transpose(dense)
    return jnp.concatenate([turned[:, r : r + 1] for r in range(dense.shape[0])], axis=0)


def partial_lse(summed, kept, column, scale, top_scr, sum_scr, out_ref):
    wide = min(WIDE, kept.shape[0])
    tiles = wide // 128

    def step(n, carry):
        right = kept[pl.ds(pl.multiple_of(n * wide, wide), wide), :]
        t = lax.dot_general(summed[...], right, NT, preferred_element_type=F32) + column
        top = jnp.max(t, axis=0, keepdims=True)
        total = jnp.sum(jnp.exp2((t - top) * scale), axis=0, keepdims=True)
        for i in range(tiles):
            top_scr[pl.ds(n * tiles + i, 1), :] = top[:, i * 128 : (i + 1) * 128]
            sum_scr[pl.ds(n * tiles + i, 1), :] = total[:, i * 128 : (i + 1) * 128]
        return carry

    lax.fori_loop(0, kept.shape[0] // wide, step, 0, unroll=2)
    part = top_scr[...] + jnp.log2(sum_scr[...]) / scale
    out_ref[...] = jnp.broadcast_to(part[None], out_ref.shape)


def first_kernel(eps, gen_showers, beam_showers, weight, out, gen_emb, beam_emb, top_scr, sum_scr):
    scale = 2.0 * LOG2E / eps[0]
    gen_emb[...] = jnp.tanh(jnp.dot(gen_showers[...], weight[...], preferred_element_type=F32)).astype(BF16)
    beam = jnp.tanh(jnp.dot(beam_showers[...], weight[...], preferred_element_type=F32)).astype(BF16)
    beam_emb[...] = beam
    beam = beam.astype(F32)
    column = -0.5 * jnp.sum(beam * beam, axis=1, keepdims=True)
    partial_lse(beam_emb, gen_emb, column, scale, top_scr, sum_scr, out)


def pass_kernel(before, now, log_count, eps, parts, summed, kept, out, half, top_scr, sum_scr):
    scale = 2.0 * LOG2E / eps[now]
    found = merged(parts, 2.0 * LOG2E / eps[before])
    dense = eps[before] * (0.5 * log_count) - found
    half[...] = dense
    partial_lse(summed, kept, as_column(dense), scale, top_scr, sum_scr, out)


def turned_kernel(showers, weight, emb_t, slope_t, square):
    act = jnp.tanh(lax.dot_general(weight[...], showers[...], (((0,), (1,)), ((), ())), preferred_element_type=F32))
    emb = act.astype(BF16)
    emb_t[...] = emb
    slope_t[...] = 2.0 * (1.0 - act * act)
    emb = emb.astype(F32)
    line = jnp.sum(emb * emb, axis=0, keepdims=True)
    for r in range(square.shape[0]):
        square[r : r + 1, :] = line[:, r * 128 : (r + 1) * 128]


def exact_dot(left, right):
    one = left.astype(BF16)
    rest = left - one.astype(F32)
    two = rest.astype(BF16)
    three = (rest - two.astype(F32)).astype(BF16)
    out = jnp.dot(jnp.concatenate([one, two, three], axis=0), right, preferred_element_type=F32)
    n = left.shape[0]
    return out[:n] + (out[n : 2 * n] + out[2 * n :])


def last_kernel(
    log_gen, log_beam, eps, parts, gen_half, gen_emb, beam_emb, gen_t, beam_t, gen_slope, beam_slope,
    gen_square, beam_square, gen_showers, beam_showers, gen_pot, beam_pot, grad, moved_gen, rows_scr, line_scr,
):
    e = eps[SWEEPS - 1]
    scale = 2.0 * LOG2E / e
    beam_half = e * (0.5 * log_gen) - merged(parts, scale)
    gen_pot[...] = 2.0 * gen_half[...] + gen_square[...]
    beam_pot[...] = 2.0 * beam_half + beam_square[...]
    shift = beam_half * scale - log_beam * LOG2E
    for r in range(shift.shape[0]):
        line_scr[:, r * 128 : (r + 1) * 128] = shift[r : r + 1, :]
    column = as_column(gen_half[...]) * scale
    moved_gen[...] = jnp.zeros_like(moved_gen)
    rows_scr[...] = jnp.zeros_like(rows_scr)
    wide = 256

    def step(n, carry):
        at = pl.ds(pl.multiple_of(n * wide, wide), wide)
        cross = lax.dot_general(gen_emb[...], beam_emb[at, :], NT, preferred_element_type=F32)
        mass = jnp.exp2(cross * scale + column + line_scr[:, at])
        plan = mass.astype(BF16)
        rows_scr[...] += mass[:, :128] + mass[:, 128:]
        col_mass = jnp.sum(mass, axis=0, keepdims=True)
        moved = jnp.dot(gen_t[...], plan, preferred_element_type=F32)
        pre = (col_mass * beam_t[:, at].astype(F32) - moved) * beam_slope[:, at]
        moved_gen[...] += lax.dot_general(beam_t[:, at], plan, NT, preferred_element_type=F32)
        return carry + exact_dot(pre, beam_showers[at, :])

    total = lax.fori_loop(0, beam_emb.shape[0] // wide, step, jnp.zeros((128, 256), F32))
    row_mass = lax.dot_general(
        jnp.ones((8, 128), F32), rows_scr[...], NT, precision=lax.Precision.HIGHEST, preferred_element_type=F32
    )[:1]
    pre = (row_mass * gen_t[...].astype(F32) - moved_gen[...]) * gen_slope[...]
    total = total + exact_dot(pre, gen_showers[...])
    grad[...] = jnp.transpose(total)


SCALARS = pl.BlockSpec(memory_space=pltpu.SMEM)
LOCAL = pl.BlockSpec(memory_space=pltpu.VMEM)


def call(kernel, operands, outs, scratch=()):
    return pl.pallas_call(
        kernel,
        out_shape=tuple(jax.ShapeDtypeStruct(*o) for o in outs),
        in_specs=[SCALARS if a.ndim == 1 else LOCAL for a in operands],
        out_specs=tuple(LOCAL for _ in outs),
        scratch_shapes=[pltpu.VMEM(*s) for s in scratch],
        compiler_params=pltpu.CompilerParams(vmem_limit_bytes=BYTES),
    )(*operands)


def swap(x, axis):
    return lax.all_to_all(x, axis, split_axis=0, concat_axis=0, tiled=True)


def on_device(gen_showers, beam_showers, embed_weight, eps_roster):
    gens, beams = lax.axis_size("gen"), lax.axis_size("beam")
    rows, columns = gen_showers.shape[0], beam_showers.shape[0]
    depth, width = embed_weight.shape
    log_gen, log_beam = math.log(rows * gens), math.log(columns * beams)
    r, c = rows // 128, columns // 128
    gen_scratch = [((r, 128), F32)] * 2
    beam_scratch = [((c, 128), F32)] * 2
    gen_parts, gen_emb, beam_emb = call(
        first_kernel,
        (eps_roster, gen_showers, beam_showers, embed_weight),
        [((beams, r, 128), F32), ((rows, width), BF16), ((columns, width), BF16)],
        gen_scratch,
    )
    gen_t, gen_slope, gen_square = call(
        turned_kernel,
        (gen_showers, embed_weight),
        [((width, rows), BF16), ((width, rows), F32), ((r, 128), F32)],
    )
    beam_t, beam_slope, beam_square = call(
        turned_kernel,
        (beam_showers, embed_weight),
        [((width, columns), BF16), ((width, columns), F32), ((c, 128), F32)],
    )
    for sweep in range(SWEEPS):
        if sweep:
            gen_parts, unused = call(
                functools.partial(pass_kernel, sweep - 1, sweep, log_gen),
                (eps_roster, beam_parts, beam_emb, gen_emb),
                [((beams, r, 128), F32), ((c, 128), F32)],
                gen_scratch,
            )
        gen_parts = swap(gen_parts, "beam")
        beam_parts, gen_half = call(
            functools.partial(pass_kernel, sweep, sweep, log_beam),
            (eps_roster, gen_parts, gen_emb, beam_emb),
            [((gens, c, 128), F32), ((r, 128), F32)],
            beam_scratch,
        )
        beam_parts = swap(beam_parts, "gen")
    gen_pot, beam_pot, grad = call(
        functools.partial(last_kernel, log_gen, log_beam),
        (
            eps_roster, beam_parts, gen_half, gen_emb, beam_emb, gen_t, beam_t, gen_slope, beam_slope,
            gen_square, beam_square, gen_showers, beam_showers,
        ),
        [((r, 128), F32), ((c, 128), F32), ((depth, width), F32)],
        [((width, rows), F32), ((rows, 128), F32), ((1, columns), F32)],
    )
    piece = swap(grad.reshape(gens, depth // gens, width), "gen").sum(0)
    piece = swap(jnp.broadcast_to(piece[None], (beams,) + piece.shape), "beam").sum(0)
    grad = swap(jnp.broadcast_to(piece[None], (gens,) + piece.shape), "gen")
    return gen_pot.reshape(rows), beam_pot.reshape(columns), grad.reshape(depth, width)


def solution(mesh):
    in_specs = (P("gen", None), P("beam", None), P(), P())
    out_specs = (P("gen"), P("beam"), P())
    return jax.shard_map(on_device, mesh=mesh, in_specs=in_specs, out_specs=out_specs, check_vma=False)
```

```python
import functools
import math

import jax
import jax.numpy as jnp
from jax import lax
from jax.experimental import pallas as pl
from jax.experimental.pallas import tpu as pltpu
from jax.sharding import PartitionSpec as P

SWEEPS = 4
LOG2E = 1.4426950408889634
BYTES = 16 * 1024 * 1024
FIRST_BYTES = 20 * 1024 * 1024
NT = (((1,), (1,)), ((), ()))
F32 = jnp.float32
BF16 = jnp.bfloat16
WIDE = 256
BLOCK = 64
DEEP = 512


def merged(parts, scale):
    count = parts.shape[0]
    top = parts[0]
    for d in range(1, count):
        top = jnp.maximum(top, parts[d])
    total = jnp.exp2((parts[0] - top) * scale)
    for d in range(1, count):
        total = total + jnp.exp2((parts[d] - top) * scale)
    return top + jnp.log2(total) / scale


def spread(dense, column):
    turned = jnp.transpose(dense)
    for r in range(dense.shape[0]):
        column[r * 128 : (r + 1) * 128, :] = jnp.broadcast_to(turned[:, r : r + 1], (128, 128))


def partial_lse(cross, column, scale, top_scr, sum_scr, out, factors=None, kernel=None):
    rows, lanes = cross.shape
    count, tiles = lanes // WIDE, WIDE // 128

    def lift(r):
        return jnp.concatenate([column[r : r + BLOCK, :]] * tiles, axis=1)

    def fold(x, op):
        return op(x.reshape(BLOCK // 8, 8, WIDE), axis=0)

    def put(scr, n, line):
        for i in range(tiles):
            scr[n * tiles + i : n * tiles + i + 1, :] = line[:, i * 128 : (i + 1) * 128]

    last = None
    for n in range(count + 1):
        new, old = slice(n * WIDE, (n + 1) * WIDE), slice((n - 1) * WIDE, n * WIDE)
        top = total = None
        for r in range(0, rows, BLOCK):
            at = slice(r, r + BLOCK)
            if n < count:
                if factors is None:
                    t = cross[at, new]
                else:
                    if r % DEEP == 0:
                        summed, kept = factors
                        made = lax.dot_general(summed[r : r + DEEP, :], kept[new, :], NT, preferred_element_type=F32)
                    t = made[r % DEEP : r % DEEP + BLOCK]
                    cross[at, new] = t
                t = fold(t + lift(r), jnp.max)
                top = t if top is None else jnp.maximum(top, t)
            if n > 0:
                p = jnp.exp2((cross[at, old] + lift(r) - last) * scale)
                if kernel is not None:
                    kernel[at, old] = p
                p = fold(p, jnp.sum)
                total = p if total is None else total + p
        if n > 0:
            put(sum_scr, n - 1, jnp.sum(total, axis=0, keepdims=True))
        if n < count:
            last = jnp.max(top, axis=0, keepdims=True)
            put(top_scr, n, last)
    part = top_scr[...] + jnp.log2(sum_scr[...]) / scale
    out[...] = jnp.broadcast_to(part[None], out.shape)


def embed(showers, weight, emb, slope):
    act = jnp.tanh(jnp.dot(showers[...], weight[...], preferred_element_type=F32))
    emb[...] = act.astype(BF16)
    slope[...] = 2.0 * (1.0 - act * act)


def first_kernel(
    eps, gen_far, beam_far, weight_far, out, gen_emb, beam_emb, gen_slope, gen_t, beam_t, gen_showers_t, beam_showers_t,
    gen_square, beam_square, beam_slope_t, column, top_scr, sum_scr, cross, beam_slope, gen_showers, beam_showers,
    weight, sems,
):
    copies = [
        pltpu.make_async_copy(src, dst, sems.at[i])
        for i, (src, dst) in enumerate(((weight_far, weight), (beam_far, beam_showers), (gen_far, gen_showers)))
    ]
    for copy in copies:
        copy.start()
    copies[0].wait()
    copies[1].wait()
    embed(beam_showers, weight, beam_emb, beam_slope)
    beam = beam_emb[...].astype(F32)
    column[...] = jnp.broadcast_to(-0.5 * jnp.sum(beam * beam, axis=1, keepdims=True), column.shape)
    copies[2].wait()
    embed(gen_showers, weight, gen_emb, gen_slope)
    partial_lse(cross, column, 2.0 * LOG2E / eps[0], top_scr, sum_scr, out, (beam_emb, gen_emb))
    turn(gen_emb, gen_showers, None, gen_t, gen_showers_t, gen_square)
    turn(beam_emb, beam_showers, beam_slope, beam_t, beam_showers_t, beam_square, beam_slope_t)


def made_kernel(before, now, log_count, eps, parts, summed, kept, out, cross, column, top_scr, sum_scr):
    found = merged(parts, 2.0 * LOG2E / eps[before])
    spread(eps[before] * (0.5 * log_count) - found, column)
    partial_lse(cross, column, 2.0 * LOG2E / eps[now], top_scr, sum_scr, out, (summed, kept))


def pass_kernel(before, now, log_count, eps, parts, cross, out, column, top_scr, sum_scr):
    found = merged(parts, 2.0 * LOG2E / eps[before])
    spread(eps[before] * (0.5 * log_count) - found, column)
    partial_lse(cross, column, 2.0 * LOG2E / eps[now], top_scr, sum_scr, out)


def kept_kernel(before, now, log_count, eps, parts, cross, out, kernel, stats, column):
    found = merged(parts, 2.0 * LOG2E / eps[before])
    spread(eps[before] * (0.5 * log_count) - found, column)
    half = stats.shape[0] // 2
    tops, sums = stats.at[pl.ds(0, half)], stats.at[pl.ds(half, half)]
    partial_lse(cross, column, 2.0 * LOG2E / eps[now], tops, sums, out, None, kernel)


def turn(emb, showers, slope, emb_t, showers_t, square, slope_t=None):
    for r in range(square.shape[0]):
        at = slice(r * 128, (r + 1) * 128)
        turned = jnp.transpose(emb[at, :])
        emb_t[:, at] = turned
        turned = turned.astype(F32)
        square[r : r + 1, :] = jnp.sum(turned * turned, axis=0, keepdims=True)
        showers_t[:, at] = jnp.transpose(showers[at, :])
        if slope_t is not None:
            slope_t[:, at] = jnp.transpose(slope[at, :])


def thirds(x, axis):
    one = x.astype(BF16)
    rest = x - one.astype(F32)
    two = rest.astype(BF16)
    return jnp.concatenate([one, two, (rest - two.astype(F32)).astype(BF16)], axis=axis)


def folded(x):
    n = x.shape[1] // 3
    return x[:, :n] + (x[:, n : 2 * n] + x[:, 2 * n :])


def last_kernel(
    log_gen, log_beam, eps, parts, gen_parts, kernel, stats, gen_emb, beam_emb, gen_t, beam_t, gen_slope, beam_slope,
    gen_square, beam_square, gen_showers_t, beam_showers_t, gen_pot, beam_pot, grad, rows_scr, moved_scr,
):
    e = eps[SWEEPS - 1]
    scale = 2.0 * LOG2E / e
    beam_half = e * (0.5 * log_gen) - merged(parts, scale)
    gen_pot[...] = e * log_beam - 2.0 * merged(gen_parts, scale) + gen_square[...]
    beam_pot[...] = 2.0 * beam_half + beam_square[...]
    count = stats.shape[0] // 2
    factor = jnp.exp2((stats[:count, :] + beam_half) * scale - log_beam * LOG2E)
    col_mass = stats[count:, :] * factor
    tiles = WIDE // 128

    def line(dense, n):
        return jnp.concatenate([dense[n * tiles + i : n * tiles + i + 1, :] for i in range(tiles)], axis=1)

    total = None
    for n in range(kernel.shape[1] // WIDE):
        at = slice(n * WIDE, (n + 1) * WIDE)
        mass = kernel[:, at] * line(factor, n)
        plan = mass.astype(BF16)
        sums = mass[:, :128]
        for i in range(1, tiles):
            sums = sums + mass[:, i * 128 : (i + 1) * 128]
        moved = jnp.dot(plan, beam_emb[at, :], preferred_element_type=F32)
        if n == 0:
            rows_scr[...] = sums
            moved_scr[...] = moved
        else:
            rows_scr[...] += sums
            moved_scr[...] += moved
        moved = jnp.dot(gen_t[...], plan, preferred_element_type=F32)
        pre = (line(col_mass, n) * beam_t[:, at].astype(F32) - moved) * beam_slope[:, at]
        part = lax.dot_general(beam_showers_t[:, at], thirds(pre, 0), NT, preferred_element_type=F32)
        total = part if total is None else total + part
    row_mass = jnp.sum(rows_scr[...], axis=1, keepdims=True)
    pre = (row_mass * gen_emb[...].astype(F32) - moved_scr[...]) * gen_slope[...]
    total = total + jnp.dot(gen_showers_t[...], thirds(pre, 1), preferred_element_type=F32)
    grad[...] = folded(total)


SCALARS = pl.BlockSpec(memory_space=pltpu.SMEM)
LOCAL = pl.BlockSpec(memory_space=pltpu.VMEM)
FAR = pl.BlockSpec(memory_space=pltpu.HBM)


def call(kernel, operands, outs, scratch=(), far=(), sems=0, limit=BYTES):
    specs = [SCALARS if a.ndim == 1 else FAR if i in far else LOCAL for i, a in enumerate(operands)]
    scratch = [pltpu.VMEM(*s) for s in scratch]
    if sems:
        scratch.append(pltpu.SemaphoreType.DMA((sems,)))
    return pl.pallas_call(
        kernel,
        out_shape=tuple(jax.ShapeDtypeStruct(*o) for o in outs),
        in_specs=specs,
        out_specs=tuple(LOCAL for _ in outs),
        scratch_shapes=scratch,
        compiler_params=pltpu.CompilerParams(vmem_limit_bytes=limit),
    )(*operands)


def swap(x, axis):
    return lax.all_to_all(x, axis, split_axis=0, concat_axis=0, tiled=True)


def on_device(gen_showers, beam_showers, embed_weight, eps_roster):
    gens, beams = lax.axis_size("gen"), lax.axis_size("beam")
    rows, columns = gen_showers.shape[0], beam_showers.shape[0]
    depth, width = embed_weight.shape
    log_gen, log_beam = math.log(rows * gens), math.log(columns * beams)
    r, c = rows // 128, columns // 128
    gen_out, beam_out = ((beams, r, 128), F32), ((gens, c, 128), F32)
    gen_scratch = [((columns, 128), F32), ((r, 128), F32), ((r, 128), F32)]
    beam_scratch = [((rows, 128), F32), ((c, 128), F32), ((c, 128), F32)]
    (
        gen_parts, gen_emb, beam_emb, gen_slope, gen_t, beam_t, gen_showers_t, beam_showers_t, gen_square, beam_square,
        beam_slope,
    ) = call(
        first_kernel,
        (eps_roster, gen_showers, beam_showers, embed_weight),
        [
            gen_out, ((rows, width), BF16), ((columns, width), BF16), ((rows, width), F32), ((width, rows), BF16),
            ((width, columns), BF16), ((depth, rows), BF16), ((depth, columns), BF16), ((r, 128), F32),
            ((c, 128), F32), ((width, columns), F32),
        ],
        gen_scratch
        + [((columns, rows), F32), ((columns, width), F32)]
        + [(a.shape, BF16) for a in (gen_showers, beam_showers, embed_weight)],
        far=(1, 2, 3),
        sems=3,
        limit=FIRST_BYTES,
    )
    gen_parts = swap(gen_parts, "beam")
    beam_parts, cross = call(
        functools.partial(made_kernel, 0, 0, log_beam),
        (eps_roster, gen_parts, gen_emb, beam_emb),
        [beam_out, ((rows, columns), F32)],
        beam_scratch,
    )
    for sweep in range(1, SWEEPS):
        beam_parts = swap(beam_parts, "gen")
        if sweep == 1:
            gen_parts, turned_cross = call(
                functools.partial(made_kernel, sweep - 1, sweep, log_gen),
                (eps_roster, beam_parts, beam_emb, gen_emb),
                [gen_out, ((columns, rows), F32)],
                gen_scratch,
            )
        else:
            (gen_parts,) = call(
                functools.partial(pass_kernel, sweep - 1, sweep, log_gen),
                (eps_roster, beam_parts, turned_cross),
                [gen_out],
                gen_scratch,
            )
        gen_parts = swap(gen_parts, "beam")
        if sweep < SWEEPS - 1:
            (beam_parts,) = call(
                functools.partial(pass_kernel, sweep, sweep, log_beam),
                (eps_roster, gen_parts, cross),
                [beam_out],
                beam_scratch,
            )
        else:
            beam_parts, kernel, stats = call(
                functools.partial(kept_kernel, sweep, sweep, log_beam),
                (eps_roster, gen_parts, cross),
                [beam_out, ((rows, columns), F32), ((2 * c, 128), F32)],
                beam_scratch[:1],
            )
    beam_parts = swap(beam_parts, "gen")
    gen_pot, beam_pot, grad = call(
        functools.partial(last_kernel, log_gen, log_beam),
        (
            eps_roster, beam_parts, gen_parts, kernel, stats, gen_emb, beam_emb, gen_t, beam_t, gen_slope, beam_slope,
            gen_square, beam_square, gen_showers_t, beam_showers_t,
        ),
        [((r, 128), F32), ((c, 128), F32), ((depth, width), F32)],
        [((rows, 128), F32), ((rows, width), F32)],
    )
    piece = swap(grad.reshape(gens, depth // gens, width), "gen").sum(0)
    piece = swap(jnp.broadcast_to(piece[None], (beams,) + piece.shape), "beam").sum(0)
    grad = swap(jnp.broadcast_to(piece[None], (gens,) + piece.shape), "gen")
    return gen_pot.reshape(rows), beam_pot.reshape(columns), grad.reshape(depth, width)


def solution(mesh):
    in_specs = (P("gen", None), P("beam", None), P(), P())
    out_specs = (P("gen"), P("beam"), P())
    return jax.shard_map(on_device, mesh=mesh, in_specs=in_specs, out_specs=out_specs, check_vma=False)
```

```python
import functools
import math

import jax
import jax.numpy as jnp
from jax import lax
from jax.experimental import pallas as pl
from jax.experimental.pallas import tpu as pltpu
from jax.sharding import PartitionSpec as P

SWEEPS = 4
LOG2E = 1.4426950408889634
BYTES = 16 * 1024 * 1024
FIRST_BYTES = 20 * 1024 * 1024
NT = (((1,), (1,)), ((), ()))
F32 = jnp.float32
BF16 = jnp.bfloat16
WIDE = 256
BLOCK = 64
DEEP = 512


def of_sweep(table, sweep):
    return table[sweep : sweep + 1, :], table[SWEEPS + sweep : SWEEPS + sweep + 1, :]


def tabled(eps, table):
    for sweep in range(SWEEPS):
        e = jnp.broadcast_to(eps[:, sweep : sweep + 1], (1, 128))
        table[sweep : sweep + 1, :] = e
        table[SWEEPS + sweep : SWEEPS + sweep + 1, :] = 2.0 * LOG2E / e


def merged(parts, e, scale):
    count = parts.shape[0]
    top = parts[0]
    for d in range(1, count):
        top = jnp.maximum(top, parts[d])
    total = jnp.exp2((parts[0] - top) * scale)
    for d in range(1, count):
        total = total + jnp.exp2((parts[d] - top) * scale)
    return top + jnp.log2(total) * (e * (0.5 / LOG2E))


def spread(dense, column):
    turned = jnp.transpose(dense)
    for r in range(dense.shape[0]):
        column[r * 128 : (r + 1) * 128, :] = jnp.broadcast_to(turned[:, r : r + 1], (128, 128))


def partial_lse(cross, column, table, sweep, top_scr, sum_scr, out, factors=None, kernel=None):
    rows, lanes = cross.shape
    count, tiles = lanes // WIDE, WIDE // 128
    e, scale = of_sweep(table, sweep)
    wide_scale = jnp.concatenate([scale] * tiles, axis=1)

    def lift(r):
        return jnp.concatenate([column[r : r + BLOCK, :]] * tiles, axis=1)

    def fold(x, op):
        return op(x.reshape(BLOCK // 8, 8, WIDE), axis=0)

    def put(scr, n, line):
        for i in range(tiles):
            scr[n * tiles + i : n * tiles + i + 1, :] = line[:, i * 128 : (i + 1) * 128]

    last = None
    for n in range(count + 1):
        new, old = slice(n * WIDE, (n + 1) * WIDE), slice((n - 1) * WIDE, n * WIDE)
        top = total = None
        for r in range(0, rows, BLOCK):
            at = slice(r, r + BLOCK)
            if n < count:
                if factors is None:
                    t = cross[at, new]
                else:
                    if r % DEEP == 0:
                        summed, kept = factors
                        made = lax.dot_general(summed[r : r + DEEP, :], kept[new, :], NT, preferred_element_type=F32)
                    t = made[r % DEEP : r % DEEP + BLOCK]
                    cross[at, new] = t
                t = fold(t + lift(r), jnp.max)
                top = t if top is None else jnp.maximum(top, t)
            if n > 0:
                p = jnp.exp2((cross[at, old] + lift(r) - last) * wide_scale)
                if kernel is not None:
                    kernel[at, old] = p
                p = fold(p, jnp.sum)
                total = p if total is None else total + p
        if n > 0:
            put(sum_scr, n - 1, jnp.sum(total, axis=0, keepdims=True))
        if n < count:
            last = jnp.max(top, axis=0, keepdims=True)
            put(top_scr, n, last)
    part = top_scr[...] + jnp.log2(sum_scr[...]) * (e * (0.5 / LOG2E))
    out[...] = jnp.broadcast_to(part[None], out.shape)


def embed(showers, weight):
    return jnp.tanh(jnp.dot(showers[...], weight[...], preferred_element_type=F32))


def first_kernel(
    eps_far, gen_far, beam_far, weight_far, out, gen_emb, beam_emb, table,
    column, top_scr, sum_scr, cross, eps, gen_showers, beam_showers, weight, sems,
):
    pairs = ((weight_far, weight), (beam_far, beam_showers), (gen_far, gen_showers), (eps_far, eps))
    copies = [pltpu.make_async_copy(src, dst, sems.at[i]) for i, (src, dst) in enumerate(pairs)]
    for copy in copies:
        copy.start()
    copies[0].wait()
    copies[1].wait()
    beam = embed(beam_showers, weight).astype(BF16)
    beam_emb[...] = beam
    beam = beam.astype(F32)
    column[...] = jnp.broadcast_to(-0.5 * jnp.sum(beam * beam, axis=1, keepdims=True), column.shape)
    copies[2].wait()
    gen_emb[...] = embed(gen_showers, weight).astype(BF16)
    copies[3].wait()
    tabled(eps, table)
    partial_lse(cross, column, table, 0, top_scr, sum_scr, out, (beam_emb, gen_emb))


def made_kernel(before, now, log_count, table, parts, summed, kept, out, cross, column, top_scr, sum_scr):
    e, scale = of_sweep(table, before)
    spread(e * (0.5 * log_count) - merged(parts, e, scale), column)
    partial_lse(cross, column, table, now, top_scr, sum_scr, out, (summed, kept))


def pass_kernel(before, now, log_count, table, parts, cross, out, column, top_scr, sum_scr):
    e, scale = of_sweep(table, before)
    spread(e * (0.5 * log_count) - merged(parts, e, scale), column)
    partial_lse(cross, column, table, now, top_scr, sum_scr, out)


def kept_kernel(before, now, log_count, table, parts, cross, out, kernel, stats, column):
    e, scale = of_sweep(table, before)
    spread(e * (0.5 * log_count) - merged(parts, e, scale), column)
    half = stats.shape[0] // 2
    tops, sums = stats.at[pl.ds(0, half)], stats.at[pl.ds(half, half)]
    partial_lse(cross, column, table, now, tops, sums, out, None, kernel)


def halves(x):
    one = x.astype(BF16)
    return jnp.concatenate([one, (x - one.astype(F32)).astype(BF16)], axis=0)


def last_kernel(
    log_gen, log_beam, table, parts, gen_parts, kernel, stats, gen_emb, beam_emb, gen_showers, beam_showers, weight,
    gen_pot, beam_pot, grad, rows_scr, moved_scr, gen_t, pre_t,
):
    e, scale = of_sweep(table, SWEEPS - 1)
    beam_half = e * (0.5 * log_gen) - merged(parts, e, scale)
    gen_half = e * (0.5 * log_beam) - merged(gen_parts, e, scale)
    count = stats.shape[0] // 2
    factor = jnp.exp2((stats[:count, :] + beam_half) * scale - log_beam * LOG2E)
    col_mass = stats[count:, :] * factor
    tiles = WIDE // 128

    def line(dense, n):
        return jnp.concatenate([dense[n * tiles + i : n * tiles + i + 1, :] for i in range(tiles)], axis=1)

    def square(turned):
        turned = turned.astype(F32)
        return jnp.sum(turned * turned, axis=0, keepdims=True)

    for r in range(gen_half.shape[0]):
        at = slice(r * 128, (r + 1) * 128)
        turned = jnp.transpose(gen_emb[at, :])
        gen_t[:, at] = turned
        gen_pot[r : r + 1, :] = 2.0 * gen_half[r : r + 1, :] + square(turned)

    total = None
    for n in range(kernel.shape[1] // WIDE):
        at = slice(n * WIDE, (n + 1) * WIDE)
        mass = kernel[:, at] * line(factor, n)
        plan = mass.astype(BF16)
        sums = mass[:, :128]
        for i in range(1, tiles):
            sums = sums + mass[:, i * 128 : (i + 1) * 128]
        moved = jnp.dot(plan, beam_emb[at, :], preferred_element_type=F32)
        if n == 0:
            rows_scr[...] = sums
            moved_scr[...] = moved
        else:
            rows_scr[...] += sums
            moved_scr[...] += moved
        moved = jnp.dot(gen_t[...], plan, preferred_element_type=F32)
        act = jnp.tanh(
            lax.dot_general(weight[...], beam_showers[at, :], (((0,), (1,)), ((), ())), preferred_element_type=F32)
        )
        beam_t = act.astype(BF16)
        for i in range(tiles):
            t = n * tiles + i
            beam_pot[t : t + 1, :] = 2.0 * beam_half[t : t + 1, :] + square(beam_t[:, i * 128 : (i + 1) * 128])
        pre = 2.0 * (line(col_mass, n) * beam_t.astype(F32) - moved) * (1.0 - act * act)
        part = jnp.dot(halves(pre), beam_showers[at, :], preferred_element_type=F32)
        total = part if total is None else total + part
    row_mass = jnp.sum(rows_scr[...], axis=1, keepdims=True)
    act = embed(gen_showers, weight)
    pre = 2.0 * (row_mass * gen_emb[...].astype(F32) - moved_scr[...]) * (1.0 - act * act)
    for r in range(gen_half.shape[0]):
        at = slice(r * 128, (r + 1) * 128)
        pre_t[:, at] = jnp.transpose(pre[at, :])
    total = total + jnp.dot(halves(pre_t[...]), gen_showers[...], preferred_element_type=F32)
    width = total.shape[0] // 2
    grad[...] = jnp.transpose(total[:width] + total[width:])


LOCAL = pl.BlockSpec(memory_space=pltpu.VMEM)
FAR = pl.BlockSpec(memory_space=pltpu.HBM)


def call(kernel, operands, outs, scratch=(), far=(), sems=0, limit=BYTES):
    specs = [FAR if i in far else LOCAL for i in range(len(operands))]
    scratch = [pltpu.VMEM(*s) for s in scratch]
    if sems:
        scratch.append(pltpu.SemaphoreType.DMA((sems,)))
    return pl.pallas_call(
        kernel,
        out_shape=tuple(jax.ShapeDtypeStruct(*o) for o in outs),
        in_specs=specs,
        out_specs=tuple(LOCAL for _ in outs),
        scratch_shapes=scratch,
        compiler_params=pltpu.CompilerParams(vmem_limit_bytes=limit),
    )(*operands)


def swap(x, axis):
    return lax.all_to_all(x, axis, split_axis=0, concat_axis=0, tiled=True)


def on_device(gen_showers, beam_showers, embed_weight, eps_roster):
    eps_roster = eps_roster.reshape(1, SWEEPS)
    gens, beams = lax.axis_size("gen"), lax.axis_size("beam")
    rows, columns = gen_showers.shape[0], beam_showers.shape[0]
    depth, width = embed_weight.shape
    log_gen, log_beam = math.log(rows * gens), math.log(columns * beams)
    r, c = rows // 128, columns // 128
    gen_out, beam_out = ((beams, r, 128), F32), ((gens, c, 128), F32)
    gen_scratch = [((columns, 128), F32), ((r, 128), F32), ((r, 128), F32)]
    beam_scratch = [((rows, 128), F32), ((c, 128), F32), ((c, 128), F32)]
    gen_parts, gen_emb, beam_emb, table = call(
        first_kernel,
        (eps_roster, gen_showers, beam_showers, embed_weight),
        [gen_out, ((rows, width), BF16), ((columns, width), BF16), ((2 * SWEEPS, 128), F32)],
        gen_scratch
        + [((columns, rows), F32), (eps_roster.shape, F32)]
        + [(a.shape, BF16) for a in (gen_showers, beam_showers, embed_weight)],
        far=(0, 1, 2, 3),
        sems=4,
        limit=FIRST_BYTES,
    )
    gen_parts = swap(gen_parts, "beam")
    beam_parts, cross = call(
        functools.partial(made_kernel, 0, 0, log_beam),
        (table, gen_parts, gen_emb, beam_emb),
        [beam_out, ((rows, columns), F32)],
        beam_scratch,
    )
    for sweep in range(1, SWEEPS):
        beam_parts = swap(beam_parts, "gen")
        if sweep == 1:
            gen_parts, turned_cross = call(
                functools.partial(made_kernel, sweep - 1, sweep, log_gen),
                (table, beam_parts, beam_emb, gen_emb),
                [gen_out, ((columns, rows), F32)],
                gen_scratch,
            )
        else:
            (gen_parts,) = call(
                functools.partial(pass_kernel, sweep - 1, sweep, log_gen),
                (table, beam_parts, turned_cross),
                [gen_out],
                gen_scratch,
            )
        gen_parts = swap(gen_parts, "beam")
        if sweep < SWEEPS - 1:
            (beam_parts,) = call(
                functools.partial(pass_kernel, sweep, sweep, log_beam),
                (table, gen_parts, cross),
                [beam_out],
                beam_scratch,
            )
        else:
            beam_parts, kernel, stats = call(
                functools.partial(kept_kernel, sweep, sweep, log_beam),
                (table, gen_parts, cross),
                [beam_out, ((rows, columns), F32), ((2 * c, 128), F32)],
                beam_scratch[:1],
            )
    beam_parts = swap(beam_parts, "gen")
    gen_pot, beam_pot, grad = call(
        functools.partial(last_kernel, log_gen, log_beam),
        (
            table, beam_parts, gen_parts, kernel, stats, gen_emb, beam_emb, gen_showers, beam_showers, embed_weight,
        ),
        [((r, 128), F32), ((c, 128), F32), ((depth, width), F32)],
        [((rows, 128), F32), ((rows, width), F32), ((width, rows), BF16), ((width, rows), F32)],
    )
    piece = swap(grad.reshape(gens, depth // gens, width), "gen").sum(0)
    piece = swap(jnp.broadcast_to(piece[None], (beams,) + piece.shape), "beam").sum(0)
    grad = swap(jnp.broadcast_to(piece[None], (gens,) + piece.shape), "gen")
    return gen_pot.reshape(rows), beam_pot.reshape(columns), grad.reshape(depth, width)


def solution(mesh):
    in_specs = (P("gen", None), P("beam", None), P(), P())
    out_specs = (P("gen"), P("beam"), P())
    return jax.shard_map(on_device, mesh=mesh, in_specs=in_specs, out_specs=out_specs, check_vma=False)
```

```python
import functools
import math

import jax
import jax.numpy as jnp
from jax import lax
from jax.experimental import pallas as pl
from jax.experimental.pallas import tpu as pltpu
from jax.sharding import PartitionSpec as P

SWEEPS = 4
LOG2E = 1.4426950408889634
BYTES = 16 * 1024 * 1024
FIRST_BYTES = 53 * 1024 * 1024
NT = (((1,), (1,)), ((), ()))
F32 = jnp.float32
BF16 = jnp.bfloat16
WIDE = 256
BLOCK = 64
DEEP = 512


def of_sweep(table, sweep):
    return table[sweep : sweep + 1, :], table[SWEEPS + sweep : SWEEPS + sweep + 1, :]


def tabled(eps, table):
    for sweep in range(SWEEPS):
        e = jnp.broadcast_to(eps[:, sweep : sweep + 1], (1, 128))
        table[sweep : sweep + 1, :] = e
        table[SWEEPS + sweep : SWEEPS + sweep + 1, :] = 2.0 * LOG2E / e


def merged(parts, e, scale):
    count = parts.shape[0]
    top = parts[0]
    for d in range(1, count):
        top = jnp.maximum(top, parts[d])
    total = jnp.exp2((parts[0] - top) * scale)
    for d in range(1, count):
        total = total + jnp.exp2((parts[d] - top) * scale)
    return top + jnp.log2(total) * (e * (0.5 / LOG2E))


def spread(dense, column):
    turned = jnp.transpose(dense)
    for r in range(dense.shape[0]):
        column[r * 128 : (r + 1) * 128, :] = jnp.broadcast_to(turned[:, r : r + 1], (128, 128))


def partial_lse(cross, column, table, sweep, top_scr, sum_scr, out, factors=None, kernel=None):
    rows, lanes = cross.shape
    count, tiles = lanes // WIDE, WIDE // 128
    e, scale = of_sweep(table, sweep)
    wide_scale = jnp.concatenate([scale] * tiles, axis=1)

    def lift(r):
        return jnp.concatenate([column[r : r + BLOCK, :]] * tiles, axis=1)

    def fold(x, op):
        return op(x.reshape(BLOCK // 8, 8, WIDE), axis=0)

    def put(scr, n, line):
        for i in range(tiles):
            scr[n * tiles + i : n * tiles + i + 1, :] = line[:, i * 128 : (i + 1) * 128]

    last = None
    for n in range(count + 1):
        new, old = slice(n * WIDE, (n + 1) * WIDE), slice((n - 1) * WIDE, n * WIDE)
        top = total = None
        for r in range(0, rows, BLOCK):
            at = slice(r, r + BLOCK)
            if n < count:
                if factors is None:
                    t = cross[at, new]
                else:
                    if r % DEEP == 0:
                        summed, kept = factors
                        made = lax.dot_general(summed[r : r + DEEP, :], kept[new, :], NT, preferred_element_type=F32)
                    t = made[r % DEEP : r % DEEP + BLOCK]
                    cross[at, new] = t
                t = fold(t + lift(r), jnp.max)
                top = t if top is None else jnp.maximum(top, t)
            if n > 0:
                p = jnp.exp2((cross[at, old] + lift(r) - last) * wide_scale)
                if kernel is not None:
                    kernel[at, old] = p
                p = fold(p, jnp.sum)
                total = p if total is None else total + p
        if n > 0:
            put(sum_scr, n - 1, jnp.sum(total, axis=0, keepdims=True))
        if n < count:
            last = jnp.max(top, axis=0, keepdims=True)
            put(top_scr, n, last)
    part = top_scr[...] + jnp.log2(sum_scr[...]) * (e * (0.5 / LOG2E))
    out[...] = jnp.broadcast_to(part[None], out.shape)


def embed(showers, weight):
    return jnp.tanh(jnp.dot(showers[...], weight[...], preferred_element_type=F32))


def first_kernel(
    eps_far, gen_far, beam_far, weight_far, out, gen_emb, beam_emb, table,
    column, top_scr, sum_scr, cross, eps, gen_showers, beam_showers, weight, sems,
):
    pairs = ((weight_far, weight), (beam_far, beam_showers), (gen_far, gen_showers), (eps_far, eps))
    copies = [pltpu.make_async_copy(src, dst, sems.at[i]) for i, (src, dst) in enumerate(pairs)]
    for copy in copies:
        copy.start()
    copies[0].wait()
    copies[1].wait()
    beam = embed(beam_showers, weight).astype(BF16)
    beam_emb[...] = beam
    beam = beam.astype(F32)
    column[...] = jnp.broadcast_to(-0.5 * jnp.sum(beam * beam, axis=1, keepdims=True), column.shape)
    copies[2].wait()
    gen_emb[...] = embed(gen_showers, weight).astype(BF16)
    copies[3].wait()
    tabled(eps, table)
    partial_lse(cross, column, table, 0, top_scr, sum_scr, out, (beam_emb, gen_emb))


def made_kernel(before, now, log_count, table, parts, summed, kept, out, cross, column, top_scr, sum_scr):
    e, scale = of_sweep(table, before)
    spread(e * (0.5 * log_count) - merged(parts, e, scale), column)
    partial_lse(cross, column, table, now, top_scr, sum_scr, out, (summed, kept))


def pass_kernel(before, now, log_count, table, parts, cross, out, column, top_scr, sum_scr):
    e, scale = of_sweep(table, before)
    spread(e * (0.5 * log_count) - merged(parts, e, scale), column)
    partial_lse(cross, column, table, now, top_scr, sum_scr, out)


def kept_kernel(before, now, log_count, table, parts, cross, out, kernel, stats, column):
    e, scale = of_sweep(table, before)
    spread(e * (0.5 * log_count) - merged(parts, e, scale), column)
    half = stats.shape[0] // 2
    tops, sums = stats.at[pl.ds(0, half)], stats.at[pl.ds(half, half)]
    partial_lse(cross, column, table, now, tops, sums, out, None, kernel)


def halves(x):
    one = x.astype(BF16)
    return jnp.concatenate([one, (x - one.astype(F32)).astype(BF16)], axis=0)


def last_kernel(
    log_gen, log_beam, table, parts, gen_parts, kernel, stats, gen_emb, beam_emb, gen_showers, beam_showers, weight,
    gen_pot, beam_pot, grad, rows_scr, moved_scr, gen_t, pre_t,
):
    e, scale = of_sweep(table, SWEEPS - 1)
    beam_half = e * (0.5 * log_gen) - merged(parts, e, scale)
    gen_half = e * (0.5 * log_beam) - merged(gen_parts, e, scale)
    count = stats.shape[0] // 2
    factor = jnp.exp2((stats[:count, :] + beam_half) * scale - log_beam * LOG2E)
    col_mass = stats[count:, :] * factor
    tiles = WIDE // 128

    def line(dense, n):
        return jnp.concatenate([dense[n * tiles + i : n * tiles + i + 1, :] for i in range(tiles)], axis=1)

    def square(turned):
        turned = turned.astype(F32)
        return jnp.sum(turned * turned, axis=0, keepdims=True)

    for r in range(gen_half.shape[0]):
        at = slice(r * 128, (r + 1) * 128)
        turned = jnp.transpose(gen_emb[at, :])
        gen_t[:, at] = turned
        gen_pot[r : r + 1, :] = 2.0 * gen_half[r : r + 1, :] + square(turned)

    total = None
    for n in range(kernel.shape[1] // WIDE):
        at = slice(n * WIDE, (n + 1) * WIDE)
        mass = kernel[:, at] * line(factor, n)
        plan = mass.astype(BF16)
        sums = mass[:, :128]
        for i in range(1, tiles):
            sums = sums + mass[:, i * 128 : (i + 1) * 128]
        moved = jnp.dot(plan, beam_emb[at, :], preferred_element_type=F32)
        if n == 0:
            rows_scr[...] = sums
            moved_scr[...] = moved
        else:
            rows_scr[...] += sums
            moved_scr[...] += moved
        moved = jnp.dot(gen_t[...], plan, preferred_element_type=F32)
        act = jnp.tanh(
            lax.dot_general(weight[...], beam_showers[at, :], (((0,), (1,)), ((), ())), preferred_element_type=F32)
        )
        beam_t = act.astype(BF16)
        for i in range(tiles):
            t = n * tiles + i
            beam_pot[t : t + 1, :] = 2.0 * beam_half[t : t + 1, :] + square(beam_t[:, i * 128 : (i + 1) * 128])
        pre = 2.0 * (line(col_mass, n) * beam_t.astype(F32) - moved) * (1.0 - act * act)
        part = jnp.dot(halves(pre), beam_showers[at, :], preferred_element_type=F32)
        total = part if total is None else total + part
    row_mass = jnp.sum(rows_scr[...], axis=1, keepdims=True)
    act = embed(gen_showers, weight)
    pre = 2.0 * (row_mass * gen_emb[...].astype(F32) - moved_scr[...]) * (1.0 - act * act)
    for r in range(gen_half.shape[0]):
        at = slice(r * 128, (r + 1) * 128)
        pre_t[:, at] = jnp.transpose(pre[at, :])
    total = total + jnp.dot(halves(pre_t[...]), gen_showers[...], preferred_element_type=F32)
    width = total.shape[0] // 2
    grad[...] = jnp.transpose(total[:width] + total[width:])


LOCAL = pl.BlockSpec(memory_space=pltpu.VMEM)
FAR = pl.BlockSpec(memory_space=pltpu.HBM)


def call(kernel, operands, outs, scratch=(), far=(), sems=0, limit=BYTES):
    specs = [FAR if i in far else LOCAL for i in range(len(operands))]
    scratch = [pltpu.VMEM(*s) for s in scratch]
    if sems:
        scratch.append(pltpu.SemaphoreType.DMA((sems,)))
    return pl.pallas_call(
        kernel,
        out_shape=tuple(jax.ShapeDtypeStruct(*o) for o in outs),
        in_specs=specs,
        out_specs=tuple(LOCAL for _ in outs),
        scratch_shapes=scratch,
        compiler_params=pltpu.CompilerParams(vmem_limit_bytes=limit),
    )(*operands)


def swap(x, axis):
    return lax.all_to_all(x, axis, split_axis=0, concat_axis=0, tiled=True)


def on_device(gen_showers, beam_showers, embed_weight, eps_roster):
    eps_roster = eps_roster.reshape(1, SWEEPS)
    gens, beams = lax.axis_size("gen"), lax.axis_size("beam")
    rows, columns = gen_showers.shape[0], beam_showers.shape[0]
    depth, width = embed_weight.shape
    log_gen, log_beam = math.log(rows * gens), math.log(columns * beams)
    r, c = rows // 128, columns // 128
    gen_out, beam_out = ((beams, r, 128), F32), ((gens, c, 128), F32)
    gen_scratch = [((columns, 128), F32), ((r, 128), F32), ((r, 128), F32)]
    beam_scratch = [((rows, 128), F32), ((c, 128), F32), ((c, 128), F32)]
    gen_parts, gen_emb, beam_emb, table = call(
        first_kernel,
        (eps_roster, gen_showers, beam_showers, embed_weight),
        [gen_out, ((rows, width), BF16), ((columns, width), BF16), ((2 * SWEEPS, 128), F32)],
        gen_scratch
        + [((columns, rows), F32), (eps_roster.shape, F32)]
        + [(a.shape, BF16) for a in (gen_showers, beam_showers, embed_weight)],
        far=(0, 1, 2, 3),
        sems=4,
        limit=FIRST_BYTES,
    )
    gen_parts = swap(gen_parts, "beam")
    beam_parts, cross = call(
        functools.partial(made_kernel, 0, 0, log_beam),
        (table, gen_parts, gen_emb, beam_emb),
        [beam_out, ((rows, columns), F32)],
        beam_scratch,
    )
    for sweep in range(1, SWEEPS):
        beam_parts = swap(beam_parts, "gen")
        if sweep == 1:
            gen_parts, turned_cross = call(
                functools.partial(made_kernel, sweep - 1, sweep, log_gen),
                (table, beam_parts, beam_emb, gen_emb),
                [gen_out, ((columns, rows), F32)],
                gen_scratch,
            )
        else:
            (gen_parts,) = call(
                functools.partial(pass_kernel, sweep - 1, sweep, log_gen),
                (table, beam_parts, turned_cross),
                [gen_out],
                gen_scratch,
            )
        gen_parts = swap(gen_parts, "beam")
        if sweep < SWEEPS - 1:
            (beam_parts,) = call(
                functools.partial(pass_kernel, sweep, sweep, log_beam),
                (table, gen_parts, cross),
                [beam_out],
                beam_scratch,
            )
        else:
            beam_parts, kernel, stats = call(
                functools.partial(kept_kernel, sweep, sweep, log_beam),
                (table, gen_parts, cross),
                [beam_out, ((rows, columns), F32), ((2 * c, 128), F32)],
                beam_scratch[:1],
            )
    beam_parts = swap(beam_parts, "gen")
    gen_pot, beam_pot, grad = call(
        functools.partial(last_kernel, log_gen, log_beam),
        (
            table, beam_parts, gen_parts, kernel, stats, gen_emb, beam_emb, gen_showers, beam_showers, embed_weight,
        ),
        [((r, 128), F32), ((c, 128), F32), ((depth, width), F32)],
        [((rows, 128), F32), ((rows, width), F32), ((width, rows), BF16), ((width, rows), F32)],
    )
    piece = swap(grad.reshape(gens, depth // gens, width), "gen").sum(0)
    piece = swap(jnp.broadcast_to(piece[None], (beams,) + piece.shape), "beam").sum(0)
    grad = swap(jnp.broadcast_to(piece[None], (gens,) + piece.shape), "gen")
    return gen_pot.reshape(rows), beam_pot.reshape(columns), grad.reshape(depth, width)


def solution(mesh):
    in_specs = (P("gen", None), P("beam", None), P(), P())
    out_specs = (P("gen"), P("beam"), P())
    return jax.shard_map(on_device, mesh=mesh, in_specs=in_specs, out_specs=out_specs, check_vma=False)
```

```python
import functools
import math

import jax
import jax.numpy as jnp
from jax import lax
from jax.experimental import pallas as pl
from jax.experimental.pallas import tpu as pltpu
from jax.sharding import PartitionSpec as P

SWEEPS = 4
LOG2E = 1.4426950408889634
BYTES = 16 * 1024 * 1024
NT = (((1,), (1,)), ((), ()))
F32 = jnp.float32
BF16 = jnp.bfloat16
WIDE = 256
BLOCK = 64
DEEP = 1024
LAST_WIDE = 512


def of_sweep(table, sweep):
    return table[sweep : sweep + 1, :], table[SWEEPS + sweep : SWEEPS + sweep + 1, :]


def tabled(eps, table):
    for sweep in range(SWEEPS):
        e = jnp.broadcast_to(eps[:, sweep : sweep + 1], (1, 128))
        table[sweep : sweep + 1, :] = e
        table[SWEEPS + sweep : SWEEPS + sweep + 1, :] = 2.0 * LOG2E / e


def merged(parts, e, scale):
    count = parts.shape[0]
    top = parts[0]
    for d in range(1, count):
        top = jnp.maximum(top, parts[d])
    total = jnp.exp2((parts[0] - top) * scale)
    for d in range(1, count):
        total = total + jnp.exp2((parts[d] - top) * scale)
    return top + jnp.log2(total) * (e * (0.5 / LOG2E))


def spread(dense, column):
    turned = jnp.transpose(dense)
    for r in range(dense.shape[0]):
        column[r * 128 : (r + 1) * 128, :] = jnp.broadcast_to(turned[:, r : r + 1], (128, 128))


def partial_lse(cross, column, table, sweep, top_scr, sum_scr, out, factors=None, kernel=None):
    rows, lanes = cross.shape
    count, tiles = lanes // WIDE, WIDE // 128
    e, scale = of_sweep(table, sweep)
    wide_scale = jnp.concatenate([scale] * tiles, axis=1)

    def lift(r):
        return jnp.concatenate([column[r : r + BLOCK, :]] * tiles, axis=1)

    def fold(x, op):
        return op(x.reshape(BLOCK // 8, 8, WIDE), axis=0)

    def put(scr, n, line):
        for i in range(tiles):
            scr[n * tiles + i : n * tiles + i + 1, :] = line[:, i * 128 : (i + 1) * 128]

    last = None
    for n in range(count + 1):
        new, old = slice(n * WIDE, (n + 1) * WIDE), slice((n - 1) * WIDE, n * WIDE)
        top = total = None
        for r in range(0, rows, BLOCK):
            at = slice(r, r + BLOCK)
            if n < count:
                if factors is None:
                    t = cross[at, new]
                else:
                    if r % DEEP == 0:
                        summed, kept = factors
                        made = lax.dot_general(summed[r : r + DEEP, :], kept[new, :], NT, preferred_element_type=F32)
                    t = made[r % DEEP : r % DEEP + BLOCK]
                    cross[at, new] = t
                t = fold(t + lift(r), jnp.max)
                top = t if top is None else jnp.maximum(top, t)
            if n > 0:
                p = jnp.exp2((cross[at, old] + lift(r) - last) * wide_scale)
                if kernel is not None:
                    kernel[at, old] = p
                p = fold(p, jnp.sum)
                total = p if total is None else total + p
        if n > 0:
            put(sum_scr, n - 1, jnp.sum(total, axis=0, keepdims=True))
        if n < count:
            last = jnp.max(top, axis=0, keepdims=True)
            put(top_scr, n, last)
    part = top_scr[...] + jnp.log2(sum_scr[...]) * (e * (0.5 / LOG2E))
    out[...] = jnp.broadcast_to(part[None], out.shape)


def embed(showers, weight):
    return jnp.tanh(jnp.dot(showers[...], weight[...], preferred_element_type=F32))


def first_kernel(
    eps_far, gen_far, beam_far, weight_far, out, cross, gen_emb, beam_emb, table,
    column, top_scr, sum_scr, eps, gen_showers, beam_showers, weight, sems,
):
    pairs = ((weight_far, weight), (beam_far, beam_showers), (gen_far, gen_showers), (eps_far, eps))
    copies = [pltpu.make_async_copy(src, dst, sems.at[i]) for i, (src, dst) in enumerate(pairs)]
    for copy in copies:
        copy.start()
    copies[0].wait()
    copies[1].wait()
    beam = embed(beam_showers, weight).astype(BF16)
    beam_emb[...] = beam
    beam = beam.astype(F32)
    column[...] = jnp.broadcast_to(-0.5 * jnp.sum(beam * beam, axis=1, keepdims=True), column.shape)
    copies[2].wait()
    gen_emb[...] = embed(gen_showers, weight).astype(BF16)
    copies[3].wait()
    tabled(eps, table)
    partial_lse(cross, column, table, 0, top_scr, sum_scr, out, (beam_emb, gen_emb))


def made_kernel(before, now, log_count, table, parts, summed, kept, out, cross, column, top_scr, sum_scr):
    e, scale = of_sweep(table, before)
    spread(e * (0.5 * log_count) - merged(parts, e, scale), column)
    partial_lse(cross, column, table, now, top_scr, sum_scr, out, (summed, kept))


def pass_kernel(before, now, log_count, table, parts, cross, out, column, top_scr, sum_scr):
    e, scale = of_sweep(table, before)
    spread(e * (0.5 * log_count) - merged(parts, e, scale), column)
    partial_lse(cross, column, table, now, top_scr, sum_scr, out)


def kept_kernel(before, now, log_count, table, parts, cross, out, kernel, stats, column):
    e, scale = of_sweep(table, before)
    spread(e * (0.5 * log_count) - merged(parts, e, scale), column)
    half = stats.shape[0] // 2
    tops, sums = stats.at[pl.ds(0, half)], stats.at[pl.ds(half, half)]
    partial_lse(cross, column, table, now, tops, sums, out, None, kernel)


def halves(x):
    one = x.astype(BF16)
    return jnp.concatenate([one, (x - one.astype(F32)).astype(BF16)], axis=0)


def last_kernel(
    log_gen, log_beam, table, parts, gen_parts, kernel, stats, gen_emb, beam_emb, gen_showers, beam_showers, weight,
    gen_pot, beam_pot, grad, rows_scr, moved_scr, gen_t, pre_t,
):
    e, scale = of_sweep(table, SWEEPS - 1)
    beam_half = e * (0.5 * log_gen) - merged(parts, e, scale)
    gen_half = e * (0.5 * log_beam) - merged(gen_parts, e, scale)
    count = stats.shape[0] // 2
    factor = jnp.exp2((stats[:count, :] + beam_half) * scale - log_beam * LOG2E)
    col_mass = stats[count:, :] * factor
    tiles = LAST_WIDE // 128

    def line(dense, n):
        return jnp.concatenate([dense[n * tiles + i : n * tiles + i + 1, :] for i in range(tiles)], axis=1)

    def square(turned):
        turned = turned.astype(F32)
        return jnp.sum(turned * turned, axis=0, keepdims=True)

    for r in range(gen_half.shape[0]):
        at = slice(r * 128, (r + 1) * 128)
        turned = jnp.transpose(gen_emb[at, :])
        gen_t[:, at] = turned
        gen_pot[r : r + 1, :] = 2.0 * gen_half[r : r + 1, :] + square(turned)

    total = None
    for n in range(kernel.shape[1] // LAST_WIDE):
        at = slice(n * LAST_WIDE, (n + 1) * LAST_WIDE)
        mass = kernel[:, at] * line(factor, n)
        plan = mass.astype(BF16)
        sums = mass[:, :128]
        for i in range(1, tiles):
            sums = sums + mass[:, i * 128 : (i + 1) * 128]
        moved = jnp.dot(plan, beam_emb[at, :], preferred_element_type=F32)
        if n == 0:
            rows_scr[...] = sums
            moved_scr[...] = moved
        else:
            rows_scr[...] += sums
            moved_scr[...] += moved
        moved = jnp.dot(gen_t[...], plan, preferred_element_type=F32)
        act = jnp.tanh(
            lax.dot_general(weight[...], beam_showers[at, :], (((0,), (1,)), ((), ())), preferred_element_type=F32)
        )
        beam_t = act.astype(BF16)
        for i in range(tiles):
            t = n * tiles + i
            beam_pot[t : t + 1, :] = 2.0 * beam_half[t : t + 1, :] + square(beam_t[:, i * 128 : (i + 1) * 128])
        pre = 2.0 * (line(col_mass, n) * beam_t.astype(F32) - moved) * (1.0 - act * act)
        part = jnp.dot(halves(pre), beam_showers[at, :], preferred_element_type=F32)
        total = part if total is None else total + part
    row_mass = jnp.sum(rows_scr[...], axis=1, keepdims=True)
    act = embed(gen_showers, weight)
    pre = 2.0 * (row_mass * gen_emb[...].astype(F32) - moved_scr[...]) * (1.0 - act * act)
    for r in range(gen_half.shape[0]):
        at = slice(r * 128, (r + 1) * 128)
        pre_t[:, at] = jnp.transpose(pre[at, :])
    total = total + jnp.dot(halves(pre_t[...]), gen_showers[...], preferred_element_type=F32)
    width = total.shape[0] // 2
    grad[...] = jnp.transpose(total[:width] + total[width:])


LOCAL = pl.BlockSpec(memory_space=pltpu.VMEM)
FAR = pl.BlockSpec(memory_space=pltpu.HBM)


def call(kernel, operands, outs, scratch=(), far=(), sems=0):
    specs = [FAR if i in far else LOCAL for i in range(len(operands))]
    operands = [pltpu.with_memory_space_constraint(a, pltpu.HBM) if i in far else a for i, a in enumerate(operands)]
    scratch = [pltpu.VMEM(*s) for s in scratch]
    if sems:
        scratch.append(pltpu.SemaphoreType.DMA((sems,)))
    return pl.pallas_call(
        kernel,
        out_shape=tuple(jax.ShapeDtypeStruct(*o) for o in outs),
        in_specs=specs,
        out_specs=tuple(LOCAL for _ in outs),
        scratch_shapes=scratch,
        compiler_params=pltpu.CompilerParams(vmem_limit_bytes=BYTES),
    )(*operands)


def swap(x, axis):
    return lax.all_to_all(x, axis, split_axis=0, concat_axis=0, tiled=True)


def on_device(gen_showers, beam_showers, embed_weight, eps_roster):
    eps_roster = eps_roster.reshape(1, SWEEPS)
    gens, beams = lax.axis_size("gen"), lax.axis_size("beam")
    rows, columns = gen_showers.shape[0], beam_showers.shape[0]
    depth, width = embed_weight.shape
    log_gen, log_beam = math.log(rows * gens), math.log(columns * beams)
    r, c = rows // 128, columns // 128
    gen_out, beam_out = ((beams, r, 128), F32), ((gens, c, 128), F32)
    gen_scratch = [((columns, 128), F32), ((r, 128), F32), ((r, 128), F32)]
    beam_scratch = [((rows, 128), F32), ((c, 128), F32), ((c, 128), F32)]
    gen_parts, turned_cross, gen_emb, beam_emb, table = call(
        first_kernel,
        (eps_roster, gen_showers, beam_showers, embed_weight),
        [gen_out, ((columns, rows), F32), ((rows, width), BF16), ((columns, width), BF16), ((2 * SWEEPS, 128), F32)],
        gen_scratch
        + [(eps_roster.shape, F32)]
        + [(a.shape, BF16) for a in (gen_showers, beam_showers, embed_weight)],
        far=(0, 1, 2, 3),
        sems=4,
    )
    gen_parts = swap(gen_parts, "beam")
    beam_parts, cross = call(
        functools.partial(made_kernel, 0, 0, log_beam),
        (table, gen_parts, gen_emb, beam_emb),
        [beam_out, ((rows, columns), F32)],
        beam_scratch,
    )
    for sweep in range(1, SWEEPS):
        beam_parts = swap(beam_parts, "gen")
        (gen_parts,) = call(
            functools.partial(pass_kernel, sweep - 1, sweep, log_gen),
            (table, beam_parts, turned_cross),
            [gen_out],
            gen_scratch,
        )
        gen_parts = swap(gen_parts, "beam")
        if sweep < SWEEPS - 1:
            (beam_parts,) = call(
                functools.partial(pass_kernel, sweep, sweep, log_beam),
                (table, gen_parts, cross),
                [beam_out],
                beam_scratch,
            )
        else:
            beam_parts, kernel, stats = call(
                functools.partial(kept_kernel, sweep, sweep, log_beam),
                (table, gen_parts, cross),
                [beam_out, ((rows, columns), F32), ((2 * c, 128), F32)],
                beam_scratch[:1],
            )
    beam_parts = swap(beam_parts, "gen")
    gen_pot, beam_pot, grad = call(
        functools.partial(last_kernel, log_gen, log_beam),
        (
            table, beam_parts, gen_parts, kernel, stats, gen_emb, beam_emb, gen_showers, beam_showers, embed_weight,
        ),
        [((r, 128), F32), ((c, 128), F32), ((depth, width), F32)],
        [((rows, 128), F32), ((rows, width), F32), ((width, rows), BF16), ((width, rows), F32)],
    )
    piece = swap(grad.reshape(gens, depth // gens, width), "gen").sum(0)
    piece = swap(jnp.broadcast_to(piece[None], (beams,) + piece.shape), "beam").sum(0)
    grad = swap(jnp.broadcast_to(piece[None], (gens,) + piece.shape), "gen")
    return gen_pot.reshape(rows), beam_pot.reshape(columns), grad.reshape(depth, width)


def solution(mesh):
    in_specs = (P("gen", None), P("beam", None), P(), P())
    out_specs = (P("gen"), P("beam"), P())
    return jax.shard_map(on_device, mesh=mesh, in_specs=in_specs, out_specs=out_specs, check_vma=False)
```

```python
import functools
import math

import jax
import jax.numpy as jnp
from jax import lax
from jax.experimental import pallas as pl
from jax.experimental.pallas import tpu as pltpu
from jax.sharding import PartitionSpec as P

SWEEPS = 4
LOG2E = 1.4426950408889634
BYTES = 16 * 1024 * 1024
NT = (((1,), (1,)), ((), ()))
F32 = jnp.float32
BF16 = jnp.bfloat16
WIDE = 256
BLOCK = 64
DEEP = 1024
LAST_WIDE = 512


def of_sweep(table, sweep):
    return table[sweep : sweep + 1, :], table[SWEEPS + sweep : SWEEPS + sweep + 1, :]


def tabled(eps, table):
    for sweep in range(SWEEPS):
        e = jnp.broadcast_to(eps[:, sweep : sweep + 1], (1, 128))
        table[sweep : sweep + 1, :] = e
        table[SWEEPS + sweep : SWEEPS + sweep + 1, :] = 2.0 * LOG2E / e


def merged(parts, e, scale):
    count = parts.shape[0]
    top = parts[0]
    for d in range(1, count):
        top = jnp.maximum(top, parts[d])
    total = jnp.exp2((parts[0] - top) * scale)
    for d in range(1, count):
        total = total + jnp.exp2((parts[d] - top) * scale)
    return top + jnp.log2(total) * (e * (0.5 / LOG2E))


def spread(dense, column):
    turned = jnp.transpose(dense)
    for r in range(dense.shape[0]):
        column[r * 128 : (r + 1) * 128, :] = jnp.broadcast_to(turned[:, r : r + 1], (128, 128))


def partial_lse(cross, column, table, sweep, top_scr, sum_scr, out, factors=None, kernel=None):
    rows, lanes = cross.shape
    count, tiles = lanes // WIDE, WIDE // 128
    e, scale = of_sweep(table, sweep)
    wide_scale = jnp.concatenate([scale] * tiles, axis=1)

    def lift(r):
        return jnp.concatenate([column[r : r + BLOCK, :]] * tiles, axis=1)

    def fold(x, op):
        return op(x.reshape(BLOCK // 8, 8, WIDE), axis=0)

    def put(scr, n, line):
        for i in range(tiles):
            scr[n * tiles + i : n * tiles + i + 1, :] = line[:, i * 128 : (i + 1) * 128]

    last = None
    for n in range(count + 1):
        new, old = slice(n * WIDE, (n + 1) * WIDE), slice((n - 1) * WIDE, n * WIDE)
        top = total = None
        for r in range(0, rows, BLOCK):
            at = slice(r, r + BLOCK)
            if n < count:
                if factors is None:
                    t = cross[at, new]
                else:
                    if r % DEEP == 0:
                        summed, kept = factors
                        made = lax.dot_general(summed[r : r + DEEP, :], kept[new, :], NT, preferred_element_type=F32)
                    t = made[r % DEEP : r % DEEP + BLOCK]
                    cross[at, new] = t
                t = fold(t + lift(r), jnp.max)
                top = t if top is None else jnp.maximum(top, t)
            if n > 0:
                p = jnp.exp2((cross[at, old] + lift(r) - last) * wide_scale)
                if kernel is not None:
                    kernel[at, old] = p
                p = fold(p, jnp.sum)
                total = p if total is None else total + p
        if n > 0:
            put(sum_scr, n - 1, jnp.sum(total, axis=0, keepdims=True))
        if n < count:
            last = jnp.max(top, axis=0, keepdims=True)
            put(top_scr, n, last)
    part = top_scr[...] + jnp.log2(sum_scr[...]) * (e * (0.5 / LOG2E))
    out[...] = jnp.broadcast_to(part[None], out.shape)


def embed(showers, weight):
    return jnp.tanh(jnp.dot(showers[...], weight[...], preferred_element_type=F32))


def first_kernel(
    eps_far, gen_far, beam_far, weight_far, out, cross, gen_emb, beam_emb, table,
    column, top_scr, sum_scr, eps, gen_showers, beam_showers, weight, sems,
):
    pairs = ((weight_far, weight), (beam_far, beam_showers), (gen_far, gen_showers), (eps_far, eps))
    copies = [pltpu.make_async_copy(src, dst, sems.at[i]) for i, (src, dst) in enumerate(pairs)]
    for copy in copies:
        copy.start()
    copies[0].wait()
    copies[1].wait()
    copies[2].wait()
    copies[3].wait()
    beam = embed(beam_showers, weight).astype(BF16)
    beam_emb[...] = beam
    beam = beam.astype(F32)
    column[...] = jnp.broadcast_to(-0.5 * jnp.sum(beam * beam, axis=1, keepdims=True), column.shape)
    gen_emb[...] = embed(gen_showers, weight).astype(BF16)
    tabled(eps, table)
    partial_lse(cross, column, table, 0, top_scr, sum_scr, out, (beam_emb, gen_emb))


def made_kernel(before, now, log_count, table, parts, summed, kept, out, cross, column, top_scr, sum_scr):
    e, scale = of_sweep(table, before)
    spread(e * (0.5 * log_count) - merged(parts, e, scale), column)
    partial_lse(cross, column, table, now, top_scr, sum_scr, out, (summed, kept))


def pass_kernel(before, now, log_count, table, parts, cross, out, column, top_scr, sum_scr):
    e, scale = of_sweep(table, before)
    spread(e * (0.5 * log_count) - merged(parts, e, scale), column)
    partial_lse(cross, column, table, now, top_scr, sum_scr, out)


def kept_kernel(before, now, log_count, table, parts, cross, out, kernel, stats, column):
    e, scale = of_sweep(table, before)
    spread(e * (0.5 * log_count) - merged(parts, e, scale), column)
    half = stats.shape[0] // 2
    tops, sums = stats.at[pl.ds(0, half)], stats.at[pl.ds(half, half)]
    partial_lse(cross, column, table, now, tops, sums, out, None, kernel)


def halves(x):
    one = x.astype(BF16)
    return jnp.concatenate([one, (x - one.astype(F32)).astype(BF16)], axis=0)


def last_kernel(
    log_gen, log_beam, table, parts, gen_parts, kernel, stats, gen_emb, beam_emb, gen_showers, beam_showers, weight,
    gen_pot, beam_pot, grad, rows_scr, moved_scr, gen_t, pre_t,
):
    e, scale = of_sweep(table, SWEEPS - 1)
    beam_half = e * (0.5 * log_gen) - merged(parts, e, scale)
    gen_half = e * (0.5 * log_beam) - merged(gen_parts, e, scale)
    count = stats.shape[0] // 2
    factor = jnp.exp2((stats[:count, :] + beam_half) * scale - log_beam * LOG2E)
    col_mass = stats[count:, :] * factor
    tiles = LAST_WIDE // 128

    def line(dense, n):
        return jnp.concatenate([dense[n * tiles + i : n * tiles + i + 1, :] for i in range(tiles)], axis=1)

    def square(turned):
        turned = turned.astype(F32)
        return jnp.sum(turned * turned, axis=0, keepdims=True)

    for r in range(gen_half.shape[0]):
        at = slice(r * 128, (r + 1) * 128)
        turned = jnp.transpose(gen_emb[at, :])
        gen_t[:, at] = turned
        gen_pot[r : r + 1, :] = 2.0 * gen_half[r : r + 1, :] + square(turned)

    total = None
    for n in range(kernel.shape[1] // LAST_WIDE):
        at = slice(n * LAST_WIDE, (n + 1) * LAST_WIDE)
        mass = kernel[:, at] * line(factor, n)
        plan = mass.astype(BF16)
        sums = mass[:, :128]
        for i in range(1, tiles):
            sums = sums + mass[:, i * 128 : (i + 1) * 128]
        moved = jnp.dot(plan, beam_emb[at, :], preferred_element_type=F32)
        if n == 0:
            rows_scr[...] = sums
            moved_scr[...] = moved
        else:
            rows_scr[...] += sums
            moved_scr[...] += moved
        moved = jnp.dot(gen_t[...], plan, preferred_element_type=F32)
        act = jnp.tanh(
            lax.dot_general(weight[...], beam_showers[at, :], (((0,), (1,)), ((), ())), preferred_element_type=F32)
        )
        beam_t = act.astype(BF16)
        for i in range(tiles):
            t = n * tiles + i
            beam_pot[t : t + 1, :] = 2.0 * beam_half[t : t + 1, :] + square(beam_t[:, i * 128 : (i + 1) * 128])
        pre = 2.0 * (line(col_mass, n) * beam_t.astype(F32) - moved) * (1.0 - act * act)
        part = jnp.dot(halves(pre), beam_showers[at, :], preferred_element_type=F32)
        total = part if total is None else total + part
    row_mass = jnp.sum(rows_scr[...], axis=1, keepdims=True)
    act = embed(gen_showers, weight)
    pre = 2.0 * (row_mass * gen_emb[...].astype(F32) - moved_scr[...]) * (1.0 - act * act)
    for r in range(gen_half.shape[0]):
        at = slice(r * 128, (r + 1) * 128)
        pre_t[:, at] = jnp.transpose(pre[at, :])
    total = total + jnp.dot(halves(pre_t[...]), gen_showers[...], preferred_element_type=F32)
    width = total.shape[0] // 2
    grad[...] = jnp.transpose(total[:width] + total[width:])


LOCAL = pl.BlockSpec(memory_space=pltpu.VMEM)
FAR = pl.BlockSpec(memory_space=pltpu.HBM)


def call(kernel, operands, outs, scratch=(), far=(), sems=0):
    specs = [FAR if i in far else LOCAL for i in range(len(operands))]
    operands = [pltpu.with_memory_space_constraint(a, pltpu.HBM) if i in far else a for i, a in enumerate(operands)]
    scratch = [pltpu.VMEM(*s) for s in scratch]
    if sems:
        scratch.append(pltpu.SemaphoreType.DMA((sems,)))
    return pl.pallas_call(
        kernel,
        out_shape=tuple(jax.ShapeDtypeStruct(*o) for o in outs),
        in_specs=specs,
        out_specs=tuple(LOCAL for _ in outs),
        scratch_shapes=scratch,
        compiler_params=pltpu.CompilerParams(vmem_limit_bytes=BYTES),
    )(*operands)


def swap(x, axis):
    return lax.all_to_all(x, axis, split_axis=0, concat_axis=0, tiled=True)


def on_device(gen_showers, beam_showers, embed_weight, eps_roster):
    eps_roster = eps_roster.reshape(1, SWEEPS)
    gens, beams = lax.axis_size("gen"), lax.axis_size("beam")
    rows, columns = gen_showers.shape[0], beam_showers.shape[0]
    depth, width = embed_weight.shape
    log_gen, log_beam = math.log(rows * gens), math.log(columns * beams)
    r, c = rows // 128, columns // 128
    gen_out, beam_out = ((beams, r, 128), F32), ((gens, c, 128), F32)
    gen_scratch = [((columns, 128), F32), ((r, 128), F32), ((r, 128), F32)]
    beam_scratch = [((rows, 128), F32), ((c, 128), F32), ((c, 128), F32)]
    gen_parts, turned_cross, gen_emb, beam_emb, table = call(
        first_kernel,
        (eps_roster, gen_showers, beam_showers, embed_weight),
        [gen_out, ((columns, rows), F32), ((rows, width), BF16), ((columns, width), BF16), ((2 * SWEEPS, 128), F32)],
        gen_scratch
        + [(eps_roster.shape, F32)]
        + [(a.shape, BF16) for a in (gen_showers, beam_showers, embed_weight)],
        far=(0, 1, 2, 3),
        sems=4,
    )
    gen_parts = swap(gen_parts, "beam")
    beam_parts, cross = call(
        functools.partial(made_kernel, 0, 0, log_beam),
        (table, gen_parts, gen_emb, beam_emb),
        [beam_out, ((rows, columns), F32)],
        beam_scratch,
    )
    for sweep in range(1, SWEEPS):
        beam_parts = swap(beam_parts, "gen")
        (gen_parts,) = call(
            functools.partial(pass_kernel, sweep - 1, sweep, log_gen),
            (table, beam_parts, turned_cross),
            [gen_out],
            gen_scratch,
        )
        gen_parts = swap(gen_parts, "beam")
        if sweep < SWEEPS - 1:
            (beam_parts,) = call(
                functools.partial(pass_kernel, sweep, sweep, log_beam),
                (table, gen_parts, cross),
                [beam_out],
                beam_scratch,
            )
        else:
            beam_parts, kernel, stats = call(
                functools.partial(kept_kernel, sweep, sweep, log_beam),
                (table, gen_parts, cross),
                [beam_out, ((rows, columns), F32), ((2 * c, 128), F32)],
                beam_scratch[:1],
            )
    beam_parts = swap(beam_parts, "gen")
    gen_pot, beam_pot, grad = call(
        functools.partial(last_kernel, log_gen, log_beam),
        (
            table, beam_parts, gen_parts, kernel, stats, gen_emb, beam_emb, gen_showers, beam_showers, embed_weight,
        ),
        [((r, 128), F32), ((c, 128), F32), ((depth, width), F32)],
        [((rows, 128), F32), ((rows, width), F32), ((width, rows), BF16), ((width, rows), F32)],
    )
    piece = swap(grad.reshape(gens, depth // gens, width), "gen").sum(0)
    piece = swap(jnp.broadcast_to(piece[None], (beams,) + piece.shape), "beam").sum(0)
    grad = swap(jnp.broadcast_to(piece[None], (gens,) + piece.shape), "gen")
    return gen_pot.reshape(rows), beam_pot.reshape(columns), grad.reshape(depth, width)


def solution(mesh):
    in_specs = (P("gen", None), P("beam", None), P(), P())
    out_specs = (P("gen"), P("beam"), P())
    return jax.shard_map(on_device, mesh=mesh, in_specs=in_specs, out_specs=out_specs, check_vma=False)
```

```python
import functools
import math

import jax
import jax.numpy as jnp
from jax import lax
from jax.experimental import pallas as pl
from jax.experimental.pallas import tpu as pltpu
from jax.sharding import PartitionSpec as P

SWEEPS = 4
LOG2E = 1.4426950408889634
BYTES = 16 * 1024 * 1024
NT = (((1,), (1,)), ((), ()))
F32 = jnp.float32
BF16 = jnp.bfloat16
WIDE = 256
BLOCK = 64
DEEP = 2048
LAST_WIDE = 512


def of_sweep(table, sweep):
    return table[sweep : sweep + 1, :], table[SWEEPS + sweep : SWEEPS + sweep + 1, :]


def tabled(eps, table):
    for sweep in range(SWEEPS):
        e = jnp.broadcast_to(eps[:, sweep : sweep + 1], (1, 128))
        table[sweep : sweep + 1, :] = e
        table[SWEEPS + sweep : SWEEPS + sweep + 1, :] = 2.0 * LOG2E / e


def merged(parts, e, scale):
    count = parts.shape[0]
    top = parts[0]
    for d in range(1, count):
        top = jnp.maximum(top, parts[d])
    total = jnp.exp2((parts[0] - top) * scale)
    for d in range(1, count):
        total = total + jnp.exp2((parts[d] - top) * scale)
    return top + jnp.log2(total) * (e * (0.5 / LOG2E))


def spread(dense, column):
    turned = jnp.transpose(dense)
    for r in range(dense.shape[0]):
        column[r * 128 : (r + 1) * 128, :] = jnp.broadcast_to(turned[:, r : r + 1], (128, 128))


def partial_lse(cross, column, table, sweep, top_scr, sum_scr, out, factors=None, kernel=None):
    rows, lanes = cross.shape
    count, tiles, deep = lanes // WIDE, WIDE // 128, min(DEEP, rows)
    e, scale = of_sweep(table, sweep)
    wide_scale = jnp.concatenate([scale] * tiles, axis=1)

    def lift(r):
        return jnp.concatenate([column[r : r + BLOCK, :]] * tiles, axis=1)

    def fold(x, op):
        return op(x.reshape(BLOCK // 8, 8, WIDE), axis=0)

    def put(scr, n, line):
        for i in range(tiles):
            scr[n * tiles + i : n * tiles + i + 1, :] = line[:, i * 128 : (i + 1) * 128]

    last = None
    for n in range(count + 1):
        new, old = slice(n * WIDE, (n + 1) * WIDE), slice((n - 1) * WIDE, n * WIDE)
        top = total = None
        for r in range(0, rows, BLOCK):
            at = slice(r, r + BLOCK)
            if n < count:
                if factors is None:
                    t = cross[at, new]
                else:
                    if r % deep == 0:
                        summed, kept = factors
                        made = lax.dot_general(summed[r : r + deep, :], kept[new, :], NT, preferred_element_type=F32)
                    t = made[r % deep : r % deep + BLOCK]
                    cross[at, new] = t
                t = fold(t + lift(r), jnp.max)
                top = t if top is None else jnp.maximum(top, t)
            if n > 0:
                p = jnp.exp2((cross[at, old] + lift(r) - last) * wide_scale)
                if kernel is not None:
                    kernel[at, old] = p
                p = fold(p, jnp.sum)
                total = p if total is None else total + p
        if n > 0:
            put(sum_scr, n - 1, jnp.sum(total, axis=0, keepdims=True))
        if n < count:
            last = jnp.max(top, axis=0, keepdims=True)
            put(top_scr, n, last)
    part = top_scr[...] + jnp.log2(sum_scr[...]) * (e * (0.5 / LOG2E))
    out[...] = jnp.broadcast_to(part[None], out.shape)


def embed(showers, weight):
    return jnp.tanh(jnp.dot(showers[...], weight[...], preferred_element_type=F32))


def first_kernel(
    eps_far, gen_far, beam_far, weight_far, out, cross, gen_emb, beam_emb, table,
    column, top_scr, sum_scr, eps, gen_showers, beam_showers, weight, sems,
):
    pairs = ((weight_far, weight), (beam_far, beam_showers), (gen_far, gen_showers), (eps_far, eps))
    copies = [pltpu.make_async_copy(src, dst, sems.at[i]) for i, (src, dst) in enumerate(pairs)]
    for copy in copies:
        copy.start()
    copies[0].wait()
    copies[1].wait()
    copies[2].wait()
    copies[3].wait()
    beam = embed(beam_showers, weight).astype(BF16)
    beam_emb[...] = beam
    beam = beam.astype(F32)
    column[...] = jnp.broadcast_to(-0.5 * jnp.sum(beam * beam, axis=1, keepdims=True), column.shape)
    gen_emb[...] = embed(gen_showers, weight).astype(BF16)
    tabled(eps, table)
    partial_lse(cross, column, table, 0, top_scr, sum_scr, out, (beam_emb, gen_emb))


def made_kernel(before, now, log_count, table, parts, summed, kept, out, cross, column, top_scr, sum_scr):
    e, scale = of_sweep(table, before)
    spread(e * (0.5 * log_count) - merged(parts, e, scale), column)
    partial_lse(cross, column, table, now, top_scr, sum_scr, out, (summed, kept))


def pass_kernel(before, now, log_count, table, parts, cross, out, column, top_scr, sum_scr):
    e, scale = of_sweep(table, before)
    spread(e * (0.5 * log_count) - merged(parts, e, scale), column)
    partial_lse(cross, column, table, now, top_scr, sum_scr, out)


def kept_kernel(before, now, log_count, table, parts, cross, out, kernel, stats, column):
    e, scale = of_sweep(table, before)
    spread(e * (0.5 * log_count) - merged(parts, e, scale), column)
    half = stats.shape[0] // 2
    tops, sums = stats.at[pl.ds(0, half)], stats.at[pl.ds(half, half)]
    partial_lse(cross, column, table, now, tops, sums, out, None, kernel)


def halves(x):
    one = x.astype(BF16)
    return jnp.concatenate([one, (x - one.astype(F32)).astype(BF16)], axis=0)


def last_kernel(
    log_gen, log_beam, table, parts, gen_parts, kernel, stats, gen_emb, beam_emb, gen_showers, beam_showers, weight,
    gen_pot, beam_pot, grad, rows_scr, moved_scr, gen_t, pre_t,
):
    e, scale = of_sweep(table, SWEEPS - 1)
    beam_half = e * (0.5 * log_gen) - merged(parts, e, scale)
    gen_half = e * (0.5 * log_beam) - merged(gen_parts, e, scale)
    count = stats.shape[0] // 2
    factor = jnp.exp2((stats[:count, :] + beam_half) * scale - log_beam * LOG2E)
    col_mass = stats[count:, :] * factor
    tiles = LAST_WIDE // 128

    def line(dense, n):
        return jnp.concatenate([dense[n * tiles + i : n * tiles + i + 1, :] for i in range(tiles)], axis=1)

    def square(turned):
        turned = turned.astype(F32)
        return jnp.sum(turned * turned, axis=0, keepdims=True)

    for r in range(gen_half.shape[0]):
        at = slice(r * 128, (r + 1) * 128)
        turned = jnp.transpose(gen_emb[at, :])
        gen_t[:, at] = turned
        gen_pot[r : r + 1, :] = 2.0 * gen_half[r : r + 1, :] + square(turned)

    total = None
    for n in range(kernel.shape[1] // LAST_WIDE):
        at = slice(n * LAST_WIDE, (n + 1) * LAST_WIDE)
        mass = kernel[:, at] * line(factor, n)
        plan = mass.astype(BF16)
        sums = mass[:, :128]
        for i in range(1, tiles):
            sums = sums + mass[:, i * 128 : (i + 1) * 128]
        moved = jnp.dot(plan, beam_emb[at, :], preferred_element_type=F32)
        if n == 0:
            rows_scr[...] = sums
            moved_scr[...] = moved
        else:
            rows_scr[...] += sums
            moved_scr[...] += moved
        moved = jnp.dot(gen_t[...], plan, preferred_element_type=F32)
        act = jnp.tanh(
            lax.dot_general(weight[...], beam_showers[at, :], (((0,), (1,)), ((), ())), preferred_element_type=F32)
        )
        beam_t = act.astype(BF16)
        for i in range(tiles):
            t = n * tiles + i
            beam_pot[t : t + 1, :] = 2.0 * beam_half[t : t + 1, :] + square(beam_t[:, i * 128 : (i + 1) * 128])
        pre = 2.0 * (line(col_mass, n) * beam_t.astype(F32) - moved) * (1.0 - act * act)
        part = jnp.dot(halves(pre), beam_showers[at, :], preferred_element_type=F32)
        total = part if total is None else total + part
    row_mass = jnp.sum(rows_scr[...], axis=1, keepdims=True)
    act = embed(gen_showers, weight)
    pre = 2.0 * (row_mass * gen_emb[...].astype(F32) - moved_scr[...]) * (1.0 - act * act)
    for r in range(gen_half.shape[0]):
        at = slice(r * 128, (r + 1) * 128)
        pre_t[:, at] = jnp.transpose(pre[at, :])
    total = total + jnp.dot(halves(pre_t[...]), gen_showers[...], preferred_element_type=F32)
    width = total.shape[0] // 2
    grad[...] = jnp.transpose(total[:width] + total[width:])


LOCAL = pl.BlockSpec(memory_space=pltpu.VMEM)
FAR = pl.BlockSpec(memory_space=pltpu.HBM)


def call(kernel, operands, outs, scratch=(), far=(), sems=0):
    specs = [FAR if i in far else LOCAL for i in range(len(operands))]
    operands = [pltpu.with_memory_space_constraint(a, pltpu.HBM) if i in far else a for i, a in enumerate(operands)]
    scratch = [pltpu.VMEM(*s) for s in scratch]
    if sems:
        scratch.append(pltpu.SemaphoreType.DMA((sems,)))
    return pl.pallas_call(
        kernel,
        out_shape=tuple(jax.ShapeDtypeStruct(*o) for o in outs),
        in_specs=specs,
        out_specs=tuple(LOCAL for _ in outs),
        scratch_shapes=scratch,
        compiler_params=pltpu.CompilerParams(vmem_limit_bytes=BYTES),
    )(*operands)


def swap(x, axis):
    return lax.all_to_all(x, axis, split_axis=0, concat_axis=0, tiled=True)


def on_device(gen_showers, beam_showers, embed_weight, eps_roster):
    eps_roster = eps_roster.reshape(1, SWEEPS)
    gens, beams = lax.axis_size("gen"), lax.axis_size("beam")
    rows, columns = gen_showers.shape[0], beam_showers.shape[0]
    depth, width = embed_weight.shape
    log_gen, log_beam = math.log(rows * gens), math.log(columns * beams)
    r, c = rows // 128, columns // 128
    gen_out, beam_out = ((beams, r, 128), F32), ((gens, c, 128), F32)
    gen_scratch = [((columns, 128), F32), ((r, 128), F32), ((r, 128), F32)]
    beam_scratch = [((rows, 128), F32), ((c, 128), F32), ((c, 128), F32)]
    gen_parts, turned_cross, gen_emb, beam_emb, table = call(
        first_kernel,
        (eps_roster, gen_showers, beam_showers, embed_weight),
        [gen_out, ((columns, rows), F32), ((rows, width), BF16), ((columns, width), BF16), ((2 * SWEEPS, 128), F32)],
        gen_scratch
        + [(eps_roster.shape, F32)]
        + [(a.shape, BF16) for a in (gen_showers, beam_showers, embed_weight)],
        far=(0, 1, 2, 3),
        sems=4,
    )
    gen_parts = swap(gen_parts, "beam")
    beam_parts, cross = call(
        functools.partial(made_kernel, 0, 0, log_beam),
        (table, gen_parts, gen_emb, beam_emb),
        [beam_out, ((rows, columns), F32)],
        beam_scratch,
    )
    for sweep in range(1, SWEEPS):
        beam_parts = swap(beam_parts, "gen")
        (gen_parts,) = call(
            functools.partial(pass_kernel, sweep - 1, sweep, log_gen),
            (table, beam_parts, turned_cross),
            [gen_out],
            gen_scratch,
        )
        gen_parts = swap(gen_parts, "beam")
        if sweep < SWEEPS - 1:
            (beam_parts,) = call(
                functools.partial(pass_kernel, sweep, sweep, log_beam),
                (table, gen_parts, cross),
                [beam_out],
                beam_scratch,
            )
        else:
            beam_parts, kernel, stats = call(
                functools.partial(kept_kernel, sweep, sweep, log_beam),
                (table, gen_parts, cross),
                [beam_out, ((rows, columns), F32), ((2 * c, 128), F32)],
                beam_scratch[:1],
            )
    beam_parts = swap(beam_parts, "gen")
    gen_pot, beam_pot, grad = call(
        functools.partial(last_kernel, log_gen, log_beam),
        (
            table, beam_parts, gen_parts, kernel, stats, gen_emb, beam_emb, gen_showers, beam_showers, embed_weight,
        ),
        [((r, 128), F32), ((c, 128), F32), ((depth, width), F32)],
        [((rows, 128), F32), ((rows, width), F32), ((width, rows), BF16), ((width, rows), F32)],
    )
    piece = swap(grad.reshape(gens, depth // gens, width), "gen").sum(0)
    piece = swap(jnp.broadcast_to(piece[None], (beams,) + piece.shape), "beam").sum(0)
    grad = swap(jnp.broadcast_to(piece[None], (gens,) + piece.shape), "gen")
    return gen_pot.reshape(rows), beam_pot.reshape(columns), grad.reshape(depth, width)


def solution(mesh):
    in_specs = (P("gen", None), P("beam", None), P(), P())
    out_specs = (P("gen"), P("beam"), P())
    return jax.shard_map(on_device, mesh=mesh, in_specs=in_specs, out_specs=out_specs, check_vma=False)
```
